32 devices in a mesh: member: 4 (over x, core), lat: 8 (over z, y).
Axes of the slice: x: 2, y: 2, z: 4, core: 2. Of those that a mesh axis runs over, the one named last changes fastest.
Arguments:
- tokens: bfloat16 [8, 16, 360, 1024], P('member', 'lat'), may hold values from -6 to 6
- weight: bfloat16 [1024, 1328], replicated, may hold values from -0.125 to 0.125
- channels: int32 [8], replicated, may hold values from 0 to 82, as said below
- band_rows: int32 [16], P('lat'), may hold values from 0 to 179
- target: float32 [8, 64, 1440], P(None, 'lat'), may hold values from -6 to 6
Outputs:
- energy: float32 [], replicated
- grad_tokens: bfloat16 [8, 16, 360, 1024], P('member', 'lat')
- grad_weight: float32 [1024, 128], P(('member', 'lat'))
The draws below stay inside these ranges and needn't reach their ends.
Inputs may be any that keep to these rules, and one draw needn't show every extreme that they name: `channels`: 8 different channel numbers.
All inputs are finite; a program needn't handle non-finite values.
Results may differ from the reference program's by a relative error of at most 0.0055.
Values may be sent and summed in bfloat16 or wider, within the bound.
A program may use at most 64 MiB of HBM per device.

```python
import math
import jax
import jax.numpy as jnp
from jax import lax

D = 1024
C_ALL = 83
SEL = 8
P_SIZE = 4
LON_P = 360
MEMBERS = 8
ROWS = 16
LAT = 64
LON = 1440


def shared_tokens(key):
    shared_key = jax.random.fold_in(key, 11)
    return jax.random.truncated_normal(shared_key, -4.0, 4.0, (ROWS, LON_P, D), jnp.float32)


def head_matrix(key):
    matrix_key = jax.random.fold_in(key, 12)
    values = jax.random.truncated_normal(matrix_key, -4.0, 4.0, (D, C_ALL * P_SIZE * P_SIZE), jnp.float32)
    return values * (1.0 / math.sqrt(float(D)))


def picked_channels(key):
    return jax.random.permutation(jax.random.fold_in(key, 13), C_ALL)[:SEL].astype(jnp.int32)


def member_spread(key):
    spread_key = jax.random.fold_in(key, 16)
    unit = jax.random.uniform(spread_key, (MEMBERS, ROWS), jnp.float32, 0.0, 1.0)
    return 0.2 + 1.6 * unit


def draw_channels(key, part):
    return picked_channels(key)


def draw_weight(key, part):
    return head_matrix(key).astype(jnp.bfloat16)


def draw_tokens(key, part):
    shared = shared_tokens(key)
    member_key = jax.random.fold_in(key, 14)
    spread = member_spread(key)[:, :, None, None]
    noise = jax.random.truncated_normal(member_key, -4.0, 4.0, (MEMBERS, ROWS, LON_P, D), jnp.float32)
    values = 0.94 * shared[None] + 0.34 * spread * noise
    return jnp.clip(values, -6.0, 6.0).astype(jnp.bfloat16)


def draw_target(key, part):
    shared = shared_tokens(key)
    matrix = head_matrix(key).astype(jnp.bfloat16).astype(jnp.float32)
    chosen = picked_channels(key)
    pixels = P_SIZE * P_SIZE
    columns = (chosen[:, None] * pixels + jnp.arange(pixels, dtype=jnp.int32)[None, :]).reshape(-1)
    selected = jnp.take(matrix, columns, axis=1)
    projected = jnp.dot(shared.reshape(ROWS * LON_P, D), selected, precision=lax.Precision.HIGHEST)
    grid = projected.reshape(ROWS, LON_P, SEL, P_SIZE, P_SIZE).transpose(2, 0, 3, 1, 4).reshape(SEL, LAT, LON)
    noise_key = jax.random.fold_in(key, 15)
    channel_level = jax.random.uniform(jax.random.fold_in(key, 17), (SEL,), jnp.float32, 0.2, 0.9)
    row_level = jax.random.uniform(jax.random.fold_in(key, 18), (LAT,), jnp.float32, 0.5, 1.5)
    level = channel_level[:, None, None] * row_level[None, :, None]
    noise = jax.random.truncated_normal(noise_key, -4.0, 4.0, (SEL, LAT, LON), jnp.float32)
    values = 0.85 * grid + level * noise
    return jnp.clip(values, -6.0, 6.0)


def place_ends(values, rng, smallest, top_value):
    spot = [jax.random.randint(jax.random.fold_in(rng, axis), (), 0, length) for axis, length in enumerate(values.shape)]
    widest = values.shape.index(max(values.shape))
    neighbour = spot[:widest] + [(spot[widest] + 1) % values.shape[widest]] + spot[widest + 1:]
    return values.at[tuple(spot)].set(smallest).at[tuple(neighbour)].set(top_value)


def setup_inputs(seed: int = 0) -> dict:
    splits = jax.random.split(jax.random.key(seed), 6)
    return {
        "tokens": draw_tokens(jax.random.fold_in(splits[5], 71), 0),
        "weight": draw_weight(jax.random.fold_in(splits[5], 71), 0),
        "channels": draw_channels(jax.random.fold_in(splits[5], 71), 0),
        "band_rows": place_ends(jax.random.randint(splits[3], (ROWS,), 0, 180), jax.random.fold_in(splits[3], 1), 0, 179).astype(jnp.int32),
        "target": draw_target(jax.random.fold_in(splits[5], 71), 0),
    }


EPSILON = 0.0001

def latitude_weights(band_rows, patch_side):
    pixel = band_rows[:, None].astype(jnp.float32) * patch_side + jnp.arange(patch_side, dtype=jnp.float32)[None, :] + 0.5
    return jnp.cos((90.0 - 0.25 * pixel) * (math.pi / 180.0))

def coefficients(gram_sums, members, loss_scale):
    diagonal = jnp.diagonal(gram_sums, axis1=1, axis2=2)
    squared_gap = diagonal[:, :, None] + diagonal[:, None, :] - 2.0 * gram_sums
    distance = jnp.sqrt(jnp.abs(squared_gap) + EPSILON)
    inverse = jnp.sign(squared_gap) / distance
    count_float = float(members)
    energy = jnp.sum(distance[:, :members, members]) / count_float - jnp.sum(distance[:, :members, :members]) / (2.0 * count_float * count_float)
    pair_terms = inverse[:, :members, :members] / (count_float * count_float)
    own_terms = inverse[:, :members, members] / count_float
    diagonal_add = own_terms - lax.optimization_barrier(jnp.sum(pair_terms, axis=2))
    member_coef = pair_terms + diagonal_add[:, :, None] * jnp.eye(members, dtype=jnp.float32)[None]
    coef = jnp.concatenate([member_coef, -own_terms[:, :, None]], axis=2) * loss_scale
    return (energy, coef)

def reference(tokens, weight, channels, band_rows, target):
    pixels = P_SIZE * P_SIZE
    columns = (channels[:, None] * pixels + jnp.arange(pixels, dtype=jnp.int32)[None, :]).reshape(-1)
    head_weight = jnp.take(weight, columns, axis=1)

    def forward(member_tokens):
        return jnp.dot(member_tokens.reshape(-1, D), head_weight, preferred_element_type=jnp.float32).astype(jnp.bfloat16)
    prediction = lax.map(forward, tokens)
    field = prediction.reshape(MEMBERS, ROWS, LON_P, SEL, P_SIZE, P_SIZE).transpose(0, 3, 1, 4, 2, 5).reshape(MEMBERS, SEL, LAT, LON)
    stacked = jnp.concatenate([field.astype(jnp.float32), target[None].astype(jnp.float32)], axis=0)
    row_weight = latitude_weights(band_rows, P_SIZE).reshape(LAT)
    weight_sum = jnp.sum(row_weight) * LON
    gram_sums = jnp.einsum('aslk,bslk->sab', stacked * row_weight[None, None, :, None], stacked, precision=lax.Precision.HIGHEST) / weight_sum
    energy, coef = coefficients(gram_sums, MEMBERS, float(MEMBERS * LAT * LON))
    combined = jnp.einsum('smb,bslk->mslk', coef, stacked, precision=lax.Precision.HIGHEST)
    gradient = (combined * (row_weight / weight_sum)[None, None, :, None]).astype(jnp.bfloat16)
    upstream = gradient.reshape(MEMBERS, SEL, ROWS, P_SIZE, LON_P, P_SIZE).transpose(0, 2, 4, 1, 3, 5).reshape(MEMBERS, ROWS * LON_P, SEL * pixels)

    def backward(member_upstream):
        return jnp.dot(member_upstream, head_weight.T, preferred_element_type=jnp.float32).astype(jnp.bfloat16)
    grad_tokens = lax.map(backward, upstream).reshape(tokens.shape)

    def accumulate(running, pair_in):
        member_tokens, member_upstream = pair_in
        return (running + jnp.dot(member_tokens.reshape(-1, D).T, member_upstream, preferred_element_type=jnp.float32), None)
    summed, _ = lax.scan(accumulate, jnp.zeros((D, SEL * pixels), jnp.float32), (tokens, upstream))
    grad_weight = summed / math.sqrt(float(MEMBERS * ROWS * LON_P))
    return (energy, grad_tokens, grad_weight)
```

```python
import functools
import math

import jax
import jax.numpy as jnp
from jax import lax
from jax.experimental import pallas as pl
from jax.experimental.pallas import tpu as pltpu
from jax.sharding import PartitionSpec as P

SEL = 8
P_SIZE = 4
PIX = P_SIZE * P_SIZE
LANES = SEL * PIX
EPSILON = 0.0001
F32 = jnp.float32
BF16 = jnp.bfloat16
HIGH = lax.Precision.HIGHEST
VMEM_LIMIT = 40 * 1024 * 1024


def round_up(value, step):
    return -(-value // step) * step


def iota(shape, axis):
    return lax.broadcasted_iota(jnp.int32, shape, axis)


def body(
    G,
    L,
    LM,
    BANDS,
    COLS,
    chan_ref,
    band_ref,
    tok_hbm,
    w_hbm,
    tgt_hbm,
    energy_ref,
    gtok_hbm,
    gw_ref,
    tok,
    wfull,
    head,
    head_t,
    tgt,
    wide,
    yal,
    wq,
    fields,
    rsum,
    msg,
    abuf,
    bbuf,
    crow,
    up,
    up_t,
    gout,
    s1,
    r1,
    own,
    s2,
    r2,
    ld_sem,
    p1_s,
    p1_r,
    x_s,
    x_r,
    i_s,
    i_r,
    ii_s,
    ii_r,
    iii_s,
    iii_r,
    a_s,
    a_r,
    b_s,
    b_r,
    r1_s,
    r1_r,
    r2_s,
    r2_r,
    out_s,
):
    X = G // 2
    M = G * LM
    ROWS = BANDS * COLS
    RP = fields.shape[1]
    CH = RP // G
    D = tok.shape[2]
    NBP = round_up(M + 1, 8)
    NL = M * NBP
    DB = D // G
    SB = DB // L
    me = lax.axis_index("member")
    lat = lax.axis_index("lat")
    xc = me // 2
    core = me % 2
    mate = me + 1 - 2 * core

    def dev(kind, index):
        return {kind: index}

    def remote(src, dst, ssem, rsem, kind, index):
        return pltpu.make_async_remote_copy(
            src_ref=src,
            dst_ref=dst,
            send_sem=ssem,
            recv_sem=rsem,
            device_id=dev(kind, index),
            device_id_type=pl.DeviceIdType.MESH,
        )

    w_copy = pltpu.make_async_copy(w_hbm, wfull, ld_sem.at[0])
    w_copy.start()
    t_copies = []
    for lm in range(LM):
        c = pltpu.make_async_copy(
            tok_hbm.at[lm], tok.at[lm, pl.ds(0, ROWS)], ld_sem.at[2 + lm]
        )
        c.start()
        t_copies.append(c)
    y_copy = pltpu.make_async_copy(tgt_hbm, tgt, ld_sem.at[1])
    y_copy.start()

    barrier = pltpu.get_barrier_semaphore()
    for o in range(1, G):
        pl.semaphore_signal(
            barrier, inc=1, device_id=dev("member", (me + o) % G), device_id_type=pl.DeviceIdType.MESH
        )
    for o in range(1, L):
        pl.semaphore_signal(
            barrier, inc=1, device_id=dev("lat", (lat + o) % L), device_id_type=pl.DeviceIdType.MESH
        )

    C = wfull.shape[1]
    lane = iota((1, LANES), 1)
    column = jnp.zeros((1, LANES), jnp.int32)
    for s in range(SEL):
        column = jnp.where(lane // PIX == s, chan_ref[s] * PIX + lane % PIX, column)
    pick = (iota((C, LANES), 0) == column).astype(F32).astype(BF16)
    if RP > ROWS:
        for lm in range(LM):
            tok[lm, pl.ds(ROWS, RP - ROWS), :] = jnp.zeros((RP - ROWS, D), BF16)
    w_copy.wait()
    head[...] = jnp.dot(wfull[...], pick, preferred_element_type=F32).astype(BF16)
    for c in t_copies:
        c.wait()
    pl.semaphore_wait(barrier, G - 1 + L - 1)

    def chunk(index):
        return pl.ds(pl.multiple_of(index * CH, 16), CH)

    def chip_rows(index):
        return pl.ds(pl.multiple_of(index * (2 * CH), 16), 2 * CH)

    def mem(device):
        return pl.ds(device * LM, LM)

    def predict(d):
        for lm in range(LM):
            fields[me * LM + lm, chunk(d), :] = jnp.dot(
                tok[lm, chunk(d), :], head[...], preferred_element_type=F32
            ).astype(BF16)

    p1 = []
    for o in [o for o in range(2, G)] + [1]:
        if o == 1:
            d = mate
        else:
            d = ((xc + o // 2) % X) * 2 + (core + o % 2) % 2
        predict(d)
        part = fields.at[mem(me), chunk(d)]
        c = remote(part, part, p1_s.at[o], p1_r.at[o], "member", d)
        c.start()
        p1.append(c)
    predict(me)

    def mate_own(o, owner):
        rows = chunk(owner) if o == 0 else chip_rows((xc + o) % X)
        part = fields.at[mem(owner), rows]
        return remote(part, part, i_s.at[o], i_r.at[o], "member", mate)

    i_c = [mate_own(o, me) for o in range(X)]

    lane8 = iota((8, LANES), 1)
    row8 = iota((8, LANES), 0)
    pixel = jnp.zeros((8, LANES), F32)
    for r in range(BANDS):
        pixel = jnp.where(row8 == r, band_ref[r].astype(F32) * P_SIZE, pixel)
    pixel = pixel + ((lane8 % PIX) // P_SIZE).astype(F32) + 0.5
    weights = jnp.cos((90.0 - 0.25 * pixel) * (math.pi / 180.0))
    root = jnp.sqrt(weights)
    for r in range(BANDS):
        wq[pl.ds(r * COLS, COLS), :] = jnp.broadcast_to(root[r : r + 1], (COLS, LANES))
    if RP > ROWS:
        wq[pl.ds(ROWS, RP - ROWS), :] = jnp.zeros((RP - ROWS, LANES), F32)
        yal[pl.ds(ROWS, RP - ROWS), :] = jnp.zeros((RP - ROWS, LANES), F32)
    weight_part = jnp.sum(jnp.where(row8 < BANDS, weights, 0.0), axis=0, keepdims=True) * (
        float(COLS) / float(G)
    )
    y_copy.wait()
    grid_rows = BANDS * P_SIZE
    KT = SEL * grid_rows
    values = tgt[...]
    high = values.astype(BF16)
    low = (values - high.astype(F32)).astype(BF16)
    k_id = iota((KT, LANES), 0)
    n_id = iota((KT, LANES), 1)
    for r in range(BANDS):
        place = (
            ((k_id // grid_rows) == (n_id // PIX))
            & ((k_id % grid_rows) == (r * P_SIZE + (n_id % PIX) // P_SIZE))
        ).astype(F32).astype(BF16)
        dims = (((0,), (0,)), ((), ()))
        wide[...] = lax.dot_general(high, place, dims, preferred_element_type=F32) + lax.dot_general(
            low, place, dims, preferred_element_type=F32
        )
        aligned = jnp.zeros((COLS, LANES), F32)
        phase = iota((COLS, LANES), 1) % P_SIZE
        for j in range(P_SIZE):
            aligned = jnp.where(phase == j, wide[pl.ds(j, COLS, stride=P_SIZE), :], aligned)
        yal[pl.ds(r * COLS, COLS), :] = aligned
    head_t[...] = head[...].astype(F32).T.astype(BF16)
    rsum[...] = jnp.zeros(rsum.shape, F32)
    rsum[pl.ds(NBP - 1 if NBP > M + 1 else 0, 1), :] = weight_part
    wslot = NBP - 1 if NBP > M + 1 else 0

    for c in p1:
        c.wait_recv()

    x_c = []
    for o in range(1, X):
        for o2 in range(X):
            if o2 != o:
                part = fields.at[mem(me), chip_rows((xc + o2) % X)]
                c = remote(part, part, x_s.at[o, o2], x_r.at[o, o2], "member", ((xc + o) % X) * 2 + core)
                c.start()
                x_c.append((o, o2, c))
    for c in i_c:
        c.start()
    ii_c = []
    for o in range(1, X):
        chip = (xc + o) % X
        part = fields.at[pl.ds(chip * (2 * LM), 2 * LM), chunk(me)]
        c = remote(part, part, ii_s.at[o], ii_r.at[o], "member", mate)
        c.start()
        ii_c.append(c)

    pairs = [(a, b) for a in range(M) for b in range(a + 1, M + 1)]
    for first in range(0, len(pairs), 36):
        group = pairs[first : first + 36]
        used = sorted({a for pair in group for a in pair})

        def gap_step(k, sums, group=group, used=used):
            start = pl.multiple_of(me * CH + k * 16, 16)
            root_rows = wq[pl.ds(start, 16), :]
            loaded = {}
            for b in used:
                if b < M:
                    loaded[b] = fields[b, pl.ds(start, 16), :].astype(F32) * root_rows
                else:
                    loaded[b] = yal[pl.ds(start, 16), :] * root_rows
            sums = list(sums)
            for half in range(2):
                part = {b: loaded[b][half * 8 : half * 8 + 8] for b in used}
                for n, (a, b) in enumerate(group):
                    delta = part[a] - part[b]
                    sums[n] = sums[n] + delta * delta
            return tuple(sums)

        zero = jnp.zeros((8, LANES), F32)
        sums = lax.fori_loop(0, CH // 16, gap_step, tuple(zero for _ in group))
        for n, (a, b) in enumerate(group):
            line = jnp.sum(sums[n], axis=0, keepdims=True)
            rsum[pl.ds(a * NBP + b, 1), :] = line
            if b < M:
                rsum[pl.ds(b * NBP + a, 1), :] = line

    channel = (iota((SEL, LANES), 0) == iota((SEL, LANES), 1) // PIX).astype(F32)
    abuf[lat] = lax.dot_general(
        channel, rsum[...], (((1,), (1,)), ((), ())), precision=HIGH, preferred_element_type=F32
    )
    a_c = []
    for o in range(1, L):
        c = remote(abuf.at[lat], abuf.at[lat], a_s.at[o], a_r.at[o], "lat", (lat + o) % L)
        c.start()
        a_c.append(c)

    iii_c = []
    for o, o2, c in x_c:
        c.wait_recv()
        chip = (xc + X - o) % X
        part = fields.at[mem(chip * 2 + core), chip_rows((chip + o2) % X)]
        q = remote(part, part, iii_s.at[o, o2], iii_r.at[o, o2], "member", mate)
        q.start()
        iii_c.append(q)

    for c in a_c:
        c.wait_recv()
    total = abuf[0]
    for l in range(1, L):
        total = total + abuf[l]
    bbuf[me] = total
    b_c = []
    for o in range(1, G):
        c = remote(bbuf.at[me], bbuf.at[me], b_s.at[o], b_r.at[o], "member", (me + o) % G)
        c.start()
        b_c.append(c)
    for c in b_c:
        c.wait_recv()
    total = bbuf[0]
    for g in range(1, G):
        total = total + bbuf[g]

    pair_lane = iota((SEL, NL), 1)
    a_id = pair_lane // NBP
    b_id = pair_lane % NBP
    weight_sum = jnp.sum(jnp.where(pair_lane == wslot, total, 0.0), axis=1, keepdims=True)
    gap = jnp.where((b_id <= M) & (a_id != b_id), total / weight_sum, 0.0)
    distance = jnp.sqrt(jnp.abs(gap) + EPSILON)
    sign = jnp.where(gap > 0.0, 1.0, jnp.where(gap < 0.0, -1.0, 0.0))
    inverse = sign / distance
    share = jnp.where(b_id < M, -1.0 / (2.0 * M * M), jnp.where(b_id == M, 1.0 / M, 0.0))
    energy_ref[...] = jnp.sum(
        jnp.sum(distance * share, axis=1, keepdims=True), axis=0, keepdims=True
    )
    crow[...] = lax.dot_general(
        inverse, channel, (((0,), (0,)), ((), ())), precision=HIGH, preferred_element_type=F32
    )
    scale = float(M * BANDS * L * P_SIZE * COLS * P_SIZE)
    one_weight = weight_sum[0:1, :]
    b_row = iota((NBP, LANES), 0)
    coefs = []
    for lm in range(LM):
        m = me * LM + lm
        inv = crow[pl.ds(pl.multiple_of(m * NBP, 8), NBP), :]
        pair_terms = jnp.where(b_row < M, inv, 0.0) * (1.0 / (M * M))
        own_terms = inv[M : M + 1] * (1.0 / M)
        add = own_terms - jnp.sum(pair_terms, axis=0, keepdims=True)
        coef = pair_terms + jnp.where(b_row == m, add, 0.0) - jnp.where(b_row == M, own_terms, 0.0)
        coefs.append(coef * (scale / one_weight))

    for o in range(X):
        mate_own(o, mate).wait_recv()
    for c in ii_c:
        c.wait_recv()
    for c in iii_c:
        c.wait_recv()

    lines = [[coefs[lm][b : b + 1] for b in range(M + 1)] for lm in range(LM)]

    def combine(k, carry):
        start = pl.multiple_of(k * 16, 16)
        root_rows = wq[pl.ds(start, 16), :]
        row_weight = root_rows * root_rows
        stacked = [fields[b, pl.ds(start, 16), :].astype(F32) for b in range(M)]
        stacked.append(yal[pl.ds(start, 16), :])
        for lm in range(LM):
            acc = stacked[0] * lines[lm][0]
            for b in range(1, M + 1):
                acc = acc + stacked[b] * lines[lm][b]
            up[lm, pl.ds(start, 16), :] = (acc * row_weight).astype(BF16)
        return carry

    lax.fori_loop(0, RP // 16, combine, 0)
    for lm in range(LM):
        up_t[lm] = up[lm].T

    def head_block(d):
        cols = pl.ds(pl.multiple_of(d * DB, 128), DB)
        acc = jnp.dot(up_t[0], tok[0, :, cols], preferred_element_type=F32)
        for lm in range(1, LM):
            acc = acc + jnp.dot(up_t[lm], tok[lm, :, cols], preferred_element_type=F32)
        return acc.T

    r1_c = []
    for o in [o for o in range(2, G)] + [1]:
        if o == 1:
            d = mate
        else:
            d = ((xc + o // 2) % X) * 2 + (core + o % 2) % 2
        s1[o] = head_block(d).astype(BF16)
        c = remote(s1.at[o], r1.at[o], r1_s.at[o], r1_r.at[o], "member", d)
        c.start()
        r1_c.append((o, c))
    total_block = head_block(me)

    parts = 3 if ROWS % 48 == 0 else 1
    step = ROWS // parts

    def back(lm, n):
        rows = pl.ds(n * step, step)
        gout[lm, rows, :] = jnp.dot(
            up[lm, rows, :], head_t[...], preferred_element_type=F32
        ).astype(BF16)
        c = pltpu.make_async_copy(
            gout.at[lm, rows], gtok_hbm.at[lm, rows], out_s.at[lm * parts + n]
        )
        c.start()
        return c

    jobs = [(lm, n) for lm in range(LM) for n in range(parts)]
    cut = len(jobs) // 2
    o_c = [back(*job) for job in jobs[:cut]]
    for o, c in r1_c:
        c.wait_recv()
    for o in range(1, G):
        total_block = total_block + r1[o].astype(F32)
    for l in range(L):
        piece = total_block[l * SB : (l + 1) * SB]
        own[l] = piece
        s2[l] = piece.astype(BF16)
    r2_c = []
    for o in range(1, L):
        l = (lat + o) % L
        c = remote(s2.at[l], r2.at[o], r2_s.at[o], r2_r.at[o], "lat", l)
        c.start()
        r2_c.append(c)
    o_c += [back(*job) for job in jobs[cut:]]
    for c in r2_c:
        c.wait_recv()
    result = own[lat]
    for o in range(1, L):
        result = result + r2[o].astype(F32)
    token_total = M * BANDS * L * COLS
    gw_ref[...] = result * (1.0 / math.sqrt(float(token_total)))

    for c in o_c:
        c.wait()
    for c in p1 + i_c + ii_c + iii_c + a_c + b_c + r2_c:
        c.wait_send()
    for _, _, c in x_c:
        c.wait_send()
    for _, c in r1_c:
        c.wait_send()


def shards(tokens, weight, channels, band_rows, target):
    LM, BANDS, COLS, D = tokens.shape
    G = lax.axis_size("member")
    L = lax.axis_size("lat")
    X = G // 2
    M = G * LM
    ROWS = BANDS * COLS
    RP = round_up(ROWS, 16 * G)
    NBP = round_up(M + 1, 8)
    NL = M * NBP
    DB = D // G
    SB = DB // L
    KT = SEL * BANDS * P_SIZE
    dma = pltpu.SemaphoreType.DMA
    parts = 3 if ROWS % 48 == 0 else 1
    any_spec = pl.BlockSpec(memory_space=pl.ANY)
    smem = pl.BlockSpec(memory_space=pltpu.SMEM)
    vmem = pl.BlockSpec(memory_space=pltpu.VMEM)
    energy, grad_tokens, grad_weight = pl.pallas_call(
        functools.partial(body, G, L, LM, BANDS, COLS),
        out_shape=(
            jax.ShapeDtypeStruct((1, 1), F32),
            jax.ShapeDtypeStruct((LM, ROWS, D), BF16),
            jax.ShapeDtypeStruct((SB, LANES), F32),
        ),
        in_specs=[smem, smem, any_spec, any_spec, any_spec],
        out_specs=(vmem, any_spec, vmem),
        scratch_shapes=[
            pltpu.VMEM((LM, RP, D), BF16),
            pltpu.VMEM(weight.shape, BF16),
            pltpu.VMEM((D, LANES), BF16),
            pltpu.VMEM((LANES, D), BF16),
            pltpu.VMEM((KT, COLS * P_SIZE), F32),
            pltpu.VMEM((COLS * P_SIZE, LANES), F32),
            pltpu.VMEM((RP, LANES), F32),
            pltpu.VMEM((RP, LANES), F32),
            pltpu.VMEM((M, RP, LANES), BF16),
            pltpu.VMEM((NL, LANES), F32),
            pltpu.VMEM((SEL, NL), F32),
            pltpu.VMEM((L, SEL, NL), F32),
            pltpu.VMEM((G, SEL, NL), F32),
            pltpu.VMEM((NL, LANES), F32),
            pltpu.VMEM((LM, RP, LANES), BF16),
            pltpu.VMEM((LM, LANES, RP), BF16),
            pltpu.VMEM((LM, ROWS, D), BF16),
            pltpu.VMEM((G, DB, LANES), BF16),
            pltpu.VMEM((G, DB, LANES), BF16),
            pltpu.VMEM((L, SB, LANES), F32),
            pltpu.VMEM((L, SB, LANES), BF16),
            pltpu.VMEM((L, SB, LANES), BF16),
            dma((2 + LM,)),
            dma((G,)),
            dma((G,)),
            dma((X, X)),
            dma((X, X)),
            dma((X,)),
            dma((X,)),
            dma((X,)),
            dma((X,)),
            dma((X, X)),
            dma((X, X)),
            dma((L,)),
            dma((L,)),
            dma((G,)),
            dma((G,)),
            dma((G,)),
            dma((G,)),
            dma((L,)),
            dma((L,)),
            dma((LM * parts,)),
        ],
        compiler_params=pltpu.CompilerParams(
            collective_id=0, has_side_effects=True, vmem_limit_bytes=VMEM_LIMIT
        ),
    )(
        channels,
        band_rows,
        tokens.reshape(LM, ROWS, D),
        weight,
        target.reshape(KT, COLS * P_SIZE),
    )
    return (energy.reshape(()), grad_tokens.reshape(tokens.shape), grad_weight)


def solution(mesh):
    placed = (P("member", "lat", None, None), P(), P(), P("lat"), P(None, "lat", None))
    return jax.shard_map(
        shards,
        mesh=mesh,
        in_specs=placed,
        out_specs=(P(), P("member", "lat", None, None), P(("member", "lat"), None)),
        check_vma=False,
    )
```

```python
import functools
import math

import jax
import jax.numpy as jnp
from jax import lax
from jax.experimental import pallas as pl
from jax.experimental.pallas import tpu as pltpu
from jax.sharding import PartitionSpec as P

SEL = 8
P_SIZE = 4
PIX = P_SIZE * P_SIZE
LANES = SEL * PIX
EPSILON = 0.0001
F32 = jnp.float32
BF16 = jnp.bfloat16
HIGH = lax.Precision.HIGHEST
VMEM_LIMIT = 121 * 512 * 1024


def round_up(value, step):
    return -(-value // step) * step


def iota(shape, axis):
    return lax.broadcasted_iota(jnp.int32, shape, axis)


def body(
    G,
    L,
    LM,
    BANDS,
    COLS,
    chan_hbm,
    band_hbm,
    tok_hbm,
    w_hbm,
    tgt_hbm,
    energy_ref,
    gout,
    gw_ref,
    chan_ref,
    band_ref,
    tok,
    wfull,
    tgt,
    wide,
    yal,
    wq,
    fields,
    rsum,
    abuf,
    bbuf,
    crow,
    up,
    head_t,
    up_t,
    s1,
    r1,
    own,
    s2,
    r2,
    ld_sem,
    p1_s,
    p1_r,
    x_s,
    x_r,
    i_s,
    i_r,
    ii_s,
    ii_r,
    iii_s,
    iii_r,
    a_s,
    a_r,
    b_s,
    b_r,
    r1_s,
    r1_r,
    r2_s,
    r2_r,
):
    X = G // 2
    M = G * LM
    ROWS = BANDS * COLS
    RP = fields.shape[1]
    CH = RP // G
    D = tok.shape[2]
    NBP = round_up(M + 1, 8)
    NL = M * NBP
    DB = D // G
    SB = DB // L
    me = lax.axis_index("member")
    lat = lax.axis_index("lat")
    xc = me // 2
    core = me % 2
    mate = me + 1 - 2 * core

    def dev(kind, index):
        return {kind: index}

    def remote(src, dst, ssem, rsem, kind, index):
        return pltpu.make_async_remote_copy(
            src_ref=src,
            dst_ref=dst,
            send_sem=ssem,
            recv_sem=rsem,
            device_id=dev(kind, index),
            device_id_type=pl.DeviceIdType.MESH,
        )

    w_copy = pltpu.make_async_copy(w_hbm, wfull, ld_sem.at[0])
    w_copy.start()
    c_copy = pltpu.make_async_copy(chan_hbm, chan_ref, ld_sem.at[2 + LM * G])
    c_copy.start()
    r_copy = pltpu.make_async_copy(band_hbm, band_ref, ld_sem.at[3 + LM * G])
    r_copy.start()
    t_copies = []
    for g in range(G):
        for lm in range(LM):
            rows = pl.ds(g * CH, min(CH, ROWS - g * CH))
            c = pltpu.make_async_copy(
                tok_hbm.at[lm, rows], tok.at[lm, rows], ld_sem.at[2 + g * LM + lm]
            )
            c.start()
            t_copies.append(c)
    y_copy = pltpu.make_async_copy(tgt_hbm, tgt, ld_sem.at[1])
    y_copy.start()

    barrier = pltpu.get_barrier_semaphore()
    for o in range(1, G):
        pl.semaphore_signal(
            barrier, inc=1, device_id=dev("member", (me + o) % G), device_id_type=pl.DeviceIdType.MESH
        )
    for o in range(1, L):
        pl.semaphore_signal(
            barrier, inc=1, device_id=dev("lat", (lat + o) % L), device_id_type=pl.DeviceIdType.MESH
        )

    if RP > ROWS:
        for lm in range(LM):
            tok[lm, pl.ds(ROWS, RP - ROWS), :] = jnp.zeros((RP - ROWS, D), BF16)
    c_copy.wait()
    r_copy.wait()
    w_copy.wait()
    for s in range(SEL):
        head_t[pl.ds(s * PIX, PIX), :] = wfull[chan_ref[s]]
    for c in t_copies:
        c.wait()
    pl.semaphore_wait(barrier, G - 1 + L - 1)

    def chunk(index):
        return pl.ds(pl.multiple_of(index * CH, 16), CH)

    def chip_rows(index):
        return pl.ds(pl.multiple_of(index * (2 * CH), 16), 2 * CH)

    def mem(device):
        return pl.ds(device * LM, LM)

    def predict(d):
        for lm in range(LM):
            fields[me * LM + lm, chunk(d), :] = lax.dot_general(
                tok[lm, chunk(d), :],
                head_t[...],
                (((1,), (1,)), ((), ())),
                preferred_element_type=F32,
            ).astype(BF16)

    p1 = []
    for o in [o for o in range(2, G)] + [1]:
        if o == 1:
            d = mate
        else:
            d = ((xc + o // 2) % X) * 2 + (core + o % 2) % 2
        predict(d)
        part = fields.at[mem(me), chunk(d)]
        c = remote(part, part, p1_s.at[o], p1_r.at[o], "member", d)
        c.start()
        p1.append(c)
    predict(me)

    def mate_own(o, owner):
        rows = chunk(owner) if o == 0 else chip_rows((xc + o) % X)
        part = fields.at[mem(owner), rows]
        return remote(part, part, i_s.at[o], i_r.at[o], "member", mate)

    i_c = [mate_own(o, me) for o in range(X)]

    lane8 = iota((8, LANES), 1)
    row8 = iota((8, LANES), 0)
    pixel = jnp.zeros((8, LANES), F32)
    for r in range(BANDS):
        pixel = jnp.where(row8 == r, band_ref[r].astype(F32) * P_SIZE, pixel)
    pixel = pixel + ((lane8 % PIX) // P_SIZE).astype(F32) + 0.5
    weights = jnp.cos((90.0 - 0.25 * pixel) * (math.pi / 180.0))
    root = jnp.sqrt(weights)
    for r in range(BANDS):
        wq[pl.ds(r * COLS, COLS), :] = jnp.broadcast_to(root[r : r + 1], (COLS, LANES))
    if RP > ROWS:
        wq[pl.ds(ROWS, RP - ROWS), :] = jnp.zeros((RP - ROWS, LANES), F32)
        yal[pl.ds(ROWS, RP - ROWS), :] = jnp.zeros((RP - ROWS, LANES), F32)
    weight_part = jnp.sum(jnp.where(row8 < BANDS, weights, 0.0), axis=0, keepdims=True) * (
        float(COLS) / float(G)
    )
    y_copy.wait()
    grid_rows = BANDS * P_SIZE
    KT = SEL * grid_rows
    values = tgt[...]
    high = values.astype(BF16)
    low = (values - high.astype(F32)).astype(BF16)
    k_id = iota((KT, LANES), 0)
    n_id = iota((KT, LANES), 1)
    for r in range(BANDS):
        place = (
            ((k_id // grid_rows) == (n_id // PIX))
            & ((k_id % grid_rows) == (r * P_SIZE + (n_id % PIX) // P_SIZE))
        ).astype(F32).astype(BF16)
        dims = (((0,), (0,)), ((), ()))
        wide[...] = lax.dot_general(high, place, dims, preferred_element_type=F32) + lax.dot_general(
            low, place, dims, preferred_element_type=F32
        )
        aligned = jnp.zeros((COLS, LANES), F32)
        phase = iota((COLS, LANES), 1) % P_SIZE
        for j in range(P_SIZE):
            aligned = jnp.where(phase == j, wide[pl.ds(j, COLS, stride=P_SIZE), :], aligned)
        yal[pl.ds(r * COLS, COLS), :] = aligned
    rsum[...] = jnp.zeros(rsum.shape, F32)
    rsum[pl.ds(NBP - 1 if NBP > M + 1 else 0, 1), :] = weight_part
    wslot = NBP - 1 if NBP > M + 1 else 0

    for c in p1[:-1]:
        c.wait_send()

    x_c = []
    for o in range(1, X):
        for o2 in range(X):
            if o2 != o:
                part = fields.at[mem(me), chip_rows((xc + o2) % X)]
                c = remote(part, part, x_s.at[o, o2], x_r.at[o, o2], "member", ((xc + o) % X) * 2 + core)
                c.start()
                x_c.append((o, o2, c))
    for c in p1:
        c.wait_recv()
    pairs = [(a, b) for a in range(M) for b in range(a + 1, M + 1)]
    for first in range(0, len(pairs), 36):
        group = pairs[first : first + 36]
        used = sorted({a for pair in group for a in pair})

        def gap_step(k, sums, group=group, used=used):
            start = pl.multiple_of(me * CH + k * 16, 16)
            root_rows = wq[pl.ds(start, 16), :]
            loaded = {}
            for b in used:
                if b < M:
                    loaded[b] = fields[b, pl.ds(start, 16), :].astype(F32) * root_rows
                else:
                    loaded[b] = yal[pl.ds(start, 16), :] * root_rows
            sums = list(sums)
            for half in range(2):
                part = {b: loaded[b][half * 8 : half * 8 + 8] for b in used}
                for n, (a, b) in enumerate(group):
                    delta = part[a] - part[b]
                    sums[n] = sums[n] + delta * delta
            return tuple(sums)

        zero = jnp.zeros((8, LANES), F32)
        sums = lax.fori_loop(0, CH // 16, gap_step, tuple(zero for _ in group))
        for n, (a, b) in enumerate(group):
            line = jnp.sum(sums[n], axis=0, keepdims=True)
            rsum[pl.ds(a * NBP + b, 1), :] = line
            if b < M:
                rsum[pl.ds(b * NBP + a, 1), :] = line

    channel = (iota((SEL, LANES), 0) == iota((SEL, LANES), 1) // PIX).astype(F32)
    abuf[lat] = lax.dot_general(
        channel, rsum[...], (((1,), (1,)), ((), ())), precision=HIGH, preferred_element_type=F32
    )
    a_c = []
    for o in range(1, L):
        c = remote(abuf.at[lat], abuf.at[lat], a_s.at[o], a_r.at[o], "lat", (lat + o) % L)
        c.start()
        a_c.append(c)

    for c in i_c:
        c.start()
    ii_c = []
    for o in range(1, X):
        chip = (xc + o) % X
        part = fields.at[pl.ds(chip * (2 * LM), 2 * LM), chunk(me)]
        c = remote(part, part, ii_s.at[o], ii_r.at[o], "member", mate)
        c.start()
        ii_c.append(c)

    for c in a_c:
        c.wait_recv()
    total = abuf[0]
    for l in range(1, L):
        total = total + abuf[l]
    bbuf[me] = total
    b_c = []
    for o in range(1, G):
        c = remote(bbuf.at[me], bbuf.at[me], b_s.at[o], b_r.at[o], "member", (me + o) % G)
        c.start()
        b_c.append(c)
    iii_c = []
    for o, o2, c in x_c:
        c.wait_recv()
        chip = (xc + X - o) % X
        part = fields.at[mem(chip * 2 + core), chip_rows((chip + o2) % X)]
        q = remote(part, part, iii_s.at[o, o2], iii_r.at[o, o2], "member", mate)
        q.start()
        iii_c.append(q)

    for c in b_c:
        c.wait_recv()
    total = bbuf[0]
    for g in range(1, G):
        total = total + bbuf[g]

    pair_lane = iota((SEL, NL), 1)
    a_id = pair_lane // NBP
    b_id = pair_lane % NBP
    weight_sum = jnp.sum(jnp.where(pair_lane == wslot, total, 0.0), axis=1, keepdims=True)
    gap = jnp.where((b_id <= M) & (a_id != b_id), total / weight_sum, 0.0)
    distance = jnp.sqrt(jnp.abs(gap) + EPSILON)
    sign = jnp.where(gap > 0.0, 1.0, jnp.where(gap < 0.0, -1.0, 0.0))
    inverse = sign / distance
    share = jnp.where(b_id < M, -1.0 / (2.0 * M * M), jnp.where(b_id == M, 1.0 / M, 0.0))
    energy_ref[...] = jnp.sum(
        jnp.sum(distance * share, axis=1, keepdims=True), axis=0, keepdims=True
    )
    crow[...] = lax.dot_general(
        inverse, channel, (((0,), (0,)), ((), ())), precision=HIGH, preferred_element_type=F32
    )
    scale = float(M * BANDS * L * P_SIZE * COLS * P_SIZE)
    one_weight = weight_sum[0:1, :]
    b_row = iota((NBP, LANES), 0)
    coefs = []
    for lm in range(LM):
        m = me * LM + lm
        inv = crow[pl.ds(pl.multiple_of(m * NBP, 8), NBP), :]
        pair_terms = jnp.where(b_row < M, inv, 0.0) * (1.0 / (M * M))
        own_terms = inv[M : M + 1] * (1.0 / M)
        add = own_terms - jnp.sum(pair_terms, axis=0, keepdims=True)
        coef = pair_terms + jnp.where(b_row == m, add, 0.0) - jnp.where(b_row == M, own_terms, 0.0)
        coefs.append(coef * (scale / one_weight))

    for o in range(X):
        mate_own(o, mate).wait_recv()
    for c in ii_c:
        c.wait_recv()
    for c in iii_c:
        c.wait_recv()

    lines = [[coefs[lm][b : b + 1] for b in range(M + 1)] for lm in range(LM)]

    def combine(k, carry):
        start = pl.multiple_of(k * 16, 16)
        root_rows = wq[pl.ds(start, 16), :]
        row_weight = root_rows * root_rows
        stacked = [fields[b, pl.ds(start, 16), :].astype(F32) for b in range(M)]
        stacked.append(yal[pl.ds(start, 16), :])
        for lm in range(LM):
            acc = stacked[0] * lines[lm][0]
            for b in range(1, M + 1):
                acc = acc + stacked[b] * lines[lm][b]
            up[lm, pl.ds(start, 16), :] = (acc * row_weight).astype(BF16)
        return carry

    lax.fori_loop(0, RP // 16, combine, 0)
    for lm in range(LM):
        up_t[lm] = up[lm].T

    def head_block(d):
        cols = pl.ds(pl.multiple_of(d * DB, 128), DB)
        acc = jnp.dot(up_t[0], tok[0, :, cols], preferred_element_type=F32)
        for lm in range(1, LM):
            acc = acc + jnp.dot(up_t[lm], tok[lm, :, cols], preferred_element_type=F32)
        return acc.T

    theirs = []
    for o in list(range(1, X)) + [0]:
        s1[o] = head_block(((xc + o) % X) * 2 + 1 - core).astype(BF16)
        c = remote(s1.at[o], r1.at[o], r1_s.at[o], r1_r.at[o], "member", mate)
        c.start()
        theirs.append(c)
    r1_c = []
    for o in range(1, X):
        block = head_block(((xc + o) % X) * 2 + core)
        theirs[o - 1].wait_recv()
        s1[X + o] = (block + r1[o].astype(F32)).astype(BF16)
        c = remote(
            s1.at[X + o], r1.at[X + o], r1_s.at[X + o], r1_r.at[X + o], "member", ((xc + o) % X) * 2 + core
        )
        c.start()
        r1_c.append((o, c))
    total_block = head_block(me)
    theirs[X - 1].wait_recv()
    total_block = total_block + r1[0].astype(F32)

    parts = 6 if ROWS % 96 == 0 else (3 if ROWS % 48 == 0 else 1)
    step = ROWS // parts

    def back(lm, n):
        rows = pl.ds(n * step, step)
        gout[lm, rows, :] = jnp.dot(
            up[lm, rows, :], head_t[...], preferred_element_type=F32
        ).astype(BF16)

    jobs = [(lm, n) for lm in range(LM) for n in range(parts)]
    cut = len(jobs) // 2
    for job in jobs[:cut]:
        back(*job)
    for o, c in r1_c:
        c.wait_recv()
    for o in range(1, X):
        total_block = total_block + r1[X + o].astype(F32)
    for l in range(L):
        piece = total_block[l * SB : (l + 1) * SB]
        own[l] = piece
        s2[l] = piece.astype(BF16)
    r2_c = []
    for o in range(1, L):
        l = (lat + o) % L
        c = remote(s2.at[l], r2.at[o], r2_s.at[o], r2_r.at[o], "lat", l)
        c.start()
        r2_c.append(c)
    for job in jobs[cut:]:
        back(*job)
    for c in r2_c:
        c.wait_recv()
    result = own[lat]
    for o in range(1, L):
        result = result + r2[o].astype(F32)
    token_total = M * BANDS * L * COLS
    gw_ref[...] = result * (1.0 / math.sqrt(float(token_total)))

    p1[-1].wait_send()
    for c in i_c + ii_c + iii_c + a_c + b_c + theirs + r2_c:
        c.wait_send()
    for _, _, c in x_c:
        c.wait_send()
    for _, c in r1_c:
        c.wait_send()


def finish(parts, energy_in, gout, gw_in, energy_hbm, gtok_hbm, gw_hbm, sems):
    LM, ROWS, _ = gout.shape
    step = ROWS // parts
    copies = []
    for lm in range(LM):
        for n in range(parts):
            rows = pl.ds(n * step, step)
            c = pltpu.make_async_copy(
                gout.at[lm, rows], gtok_hbm.at[lm, rows], sems.at[lm * parts + n]
            )
            c.start()
            copies.append(c)
    for n, (src, dst) in enumerate([(energy_in, energy_hbm), (gw_in, gw_hbm)]):
        c = pltpu.make_async_copy(src, dst, sems.at[LM * parts + n])
        c.start()
        copies.append(c)
    for c in copies:
        c.wait()


def shards(tokens, weight, channels, band_rows, target):
    LM, BANDS, COLS, D = tokens.shape
    G = lax.axis_size("member")
    L = lax.axis_size("lat")
    X = G // 2
    M = G * LM
    ROWS = BANDS * COLS
    RP = round_up(ROWS, 16 * G)
    NBP = round_up(M + 1, 8)
    NL = M * NBP
    DB = D // G
    SB = DB // L
    KT = SEL * BANDS * P_SIZE
    dma = pltpu.SemaphoreType.DMA
    parts = 3 if ROWS % 48 == 0 else 1
    hbm = pl.BlockSpec(memory_space=pltpu.HBM)
    vmem = pl.BlockSpec(memory_space=pltpu.VMEM)
    energy, gout, grad_weight = pl.pallas_call(
        functools.partial(body, G, L, LM, BANDS, COLS),
        out_shape=(
            pltpu.VMEM((1, 1), F32),
            pltpu.VMEM((LM, ROWS, D), BF16),
            pltpu.VMEM((SB, LANES), F32),
        ),
        in_specs=[hbm, hbm, hbm, hbm, hbm],
        out_specs=(vmem, vmem, vmem),
        scratch_shapes=[
            pltpu.SMEM(channels.shape, jnp.int32),
            pltpu.SMEM(band_rows.shape, jnp.int32),
            pltpu.VMEM((LM, RP, D), BF16),
            pltpu.VMEM((weight.shape[1] // PIX, PIX, D), BF16),
            pltpu.VMEM((KT, COLS * P_SIZE), F32),
            pltpu.VMEM((COLS * P_SIZE, LANES), F32),
            pltpu.VMEM((RP, LANES), F32),
            pltpu.VMEM((RP, LANES), F32),
            pltpu.VMEM((M, RP, LANES), BF16),
            pltpu.VMEM((NL, LANES), F32),
            pltpu.VMEM((L, SEL, NL), F32),
            pltpu.VMEM((G, SEL, NL), F32),
            pltpu.VMEM((NL, LANES), F32),
            pltpu.VMEM((LM, RP, LANES), BF16),
            pltpu.VMEM((LANES, D), BF16),
            pltpu.VMEM((LM, LANES, RP), BF16),
            pltpu.VMEM((G, DB, LANES), BF16),
            pltpu.VMEM((G, DB, LANES), BF16),
            pltpu.VMEM((L, SB, LANES), F32),
            pltpu.VMEM((L, SB, LANES), BF16),
            pltpu.VMEM((L, SB, LANES), BF16),
            dma((4 + LM * G,)),
            dma((G,)),
            dma((G,)),
            dma((X, X)),
            dma((X, X)),
            dma((X,)),
            dma((X,)),
            dma((X,)),
            dma((X,)),
            dma((X, X)),
            dma((X, X)),
            dma((L,)),
            dma((L,)),
            dma((G,)),
            dma((G,)),
            dma((G,)),
            dma((G,)),
            dma((L,)),
            dma((L,)),
        ],
        compiler_params=pltpu.CompilerParams(
            collective_id=0, has_side_effects=True, vmem_limit_bytes=VMEM_LIMIT
        ),
    )(
        channels,
        band_rows,
        tokens.reshape(LM, ROWS, D),
        weight.T.reshape(weight.shape[1] // PIX, PIX, D),
        target.reshape(KT, COLS * P_SIZE),
    )
    energy, grad_tokens, grad_weight = pl.pallas_call(
        functools.partial(finish, parts),
        out_shape=(
            jax.ShapeDtypeStruct((1, 1), F32),
            jax.ShapeDtypeStruct((LM, ROWS, D), BF16),
            jax.ShapeDtypeStruct((SB, LANES), F32),
        ),
        in_specs=[vmem] * 3,
        out_specs=(hbm, hbm, hbm),
        scratch_shapes=[dma((LM * parts + 2,))],
        compiler_params=pltpu.CompilerParams(vmem_limit_bytes=4 * 1024 * 1024),
    )(energy, gout, grad_weight)
    return (energy.reshape(()), grad_tokens.reshape(tokens.shape), grad_weight)


def solution(mesh):
    placed = (P("member", "lat", None, None), P(), P(), P("lat"), P(None, "lat", None))
    return jax.shard_map(
        shards,
        mesh=mesh,
        in_specs=placed,
        out_specs=(P(), P("member", "lat", None, None), P(("member", "lat"), None)),
        check_vma=False,
    )
```

```python
import functools
import math

import jax
import jax.numpy as jnp
from jax import lax
from jax.experimental import pallas as pl
from jax.experimental.pallas import tpu as pltpu
from jax.sharding import PartitionSpec as P

SEL = 8
P_SIZE = 4
PIX = P_SIZE * P_SIZE
LANES = SEL * PIX
EPSILON = 0.0001
F32 = jnp.float32
BF16 = jnp.bfloat16
HIGH = lax.Precision.HIGHEST
VMEM_LIMIT = 121 * 512 * 1024


def round_up(value, step):
    return -(-value // step) * step


def iota(shape, axis):
    return lax.broadcasted_iota(jnp.int32, shape, axis)


def body(
    G,
    L,
    LM,
    BANDS,
    COLS,
    chan_hbm,
    band_hbm,
    tok_hbm,
    w_hbm,
    tgt_hbm,
    energy_ref,
    gout,
    gw_ref,
    chan_ref,
    band_ref,
    tok,
    wfull,
    tgt,
    wide,
    yal,
    wq,
    fields,
    rsum,
    abuf,
    bbuf,
    crow,
    up,
    head_t,
    up_t,
    s1,
    r1,
    own,
    s2,
    r2,
    ld_sem,
    p1_s,
    p1_r,
    x_s,
    x_r,
    i_s,
    i_r,
    ii_s,
    ii_r,
    iii_s,
    iii_r,
    a_s,
    a_r,
    b_s,
    b_r,
    r1_s,
    r1_r,
    r2_s,
    r2_r,
):
    X = G // 2
    M = G * LM
    ROWS = BANDS * COLS
    RP = fields.shape[1]
    CH = RP // G
    D = tok.shape[2]
    NBP = round_up(M + 1, 8)
    NL = M * NBP
    DB = D // G
    SB = DB // L
    me = lax.axis_index("member")
    lat = lax.axis_index("lat")
    xc = me // 2
    core = me % 2
    mate = me + 1 - 2 * core

    def dev(kind, index):
        return {kind: index}

    def remote(src, dst, ssem, rsem, kind, index):
        return pltpu.make_async_remote_copy(
            src_ref=src,
            dst_ref=dst,
            send_sem=ssem,
            recv_sem=rsem,
            device_id=dev(kind, index),
            device_id_type=pl.DeviceIdType.MESH,
        )

    w_copy = pltpu.make_async_copy(w_hbm, wfull, ld_sem.at[0])
    w_copy.start()
    c_copy = pltpu.make_async_copy(chan_hbm, chan_ref, ld_sem.at[2 + LM * G])
    c_copy.start()
    r_copy = pltpu.make_async_copy(band_hbm, band_ref, ld_sem.at[3 + LM * G])
    r_copy.start()
    t_copies = []
    for g in range(G):
        for lm in range(LM):
            rows = pl.ds(g * CH, min(CH, ROWS - g * CH))
            c = pltpu.make_async_copy(
                tok_hbm.at[lm, rows], tok.at[lm, rows], ld_sem.at[2 + g * LM + lm]
            )
            c.start()
            t_copies.append(c)
    y_copy = pltpu.make_async_copy(tgt_hbm, tgt, ld_sem.at[1])
    y_copy.start()

    barrier = pltpu.get_barrier_semaphore()
    for o in range(1, G):
        pl.semaphore_signal(
            barrier, inc=1, device_id=dev("member", (me + o) % G), device_id_type=pl.DeviceIdType.MESH
        )
    for o in range(1, L):
        for ox in range(X):
            pl.semaphore_signal(
                barrier,
                inc=1,
                device_id={"member": ((xc + ox) % X) * 2 + core, "lat": (lat + o) % L},
                device_id_type=pl.DeviceIdType.MESH,
            )

    if RP > ROWS:
        for lm in range(LM):
            tok[lm, pl.ds(ROWS, RP - ROWS), :] = jnp.zeros((RP - ROWS, D), BF16)
    c_copy.wait()
    r_copy.wait()
    w_copy.wait()
    for s in range(SEL):
        head_t[pl.ds(s * PIX, PIX), :] = wfull[chan_ref[s]]
    for c in t_copies:
        c.wait()
    pl.semaphore_wait(barrier, G - 1 + (L - 1) * X)

    def chunk(index):
        return pl.ds(pl.multiple_of(index * CH, 16), CH)

    def chip_rows(index):
        return pl.ds(pl.multiple_of(index * (2 * CH), 16), 2 * CH)

    def mem(device):
        return pl.ds(device * LM, LM)

    def predict(d):
        for lm in range(LM):
            fields[me * LM + lm, chunk(d), :] = lax.dot_general(
                tok[lm, chunk(d), :],
                head_t[...],
                (((1,), (1,)), ((), ())),
                preferred_element_type=F32,
            ).astype(BF16)

    p1 = []
    for o in [o for o in range(2, G)] + [1]:
        if o == 1:
            d = mate
        else:
            d = ((xc + o // 2) % X) * 2 + (core + o % 2) % 2
        predict(d)
        part = fields.at[mem(me), chunk(d)]
        c = remote(part, part, p1_s.at[o], p1_r.at[o], "member", d)
        c.start()
        p1.append(c)
    predict(me)

    def mate_own(o, owner):
        rows = chunk(owner) if o == 0 else chip_rows((xc + o) % X)
        part = fields.at[mem(owner), rows]
        return remote(part, part, i_s.at[o], i_r.at[o], "member", mate)

    i_c = [mate_own(o, me) for o in range(X)]

    lane8 = iota((8, LANES), 1)
    row8 = iota((8, LANES), 0)
    pixel = jnp.zeros((8, LANES), F32)
    for r in range(BANDS):
        pixel = jnp.where(row8 == r, band_ref[r].astype(F32) * P_SIZE, pixel)
    pixel = pixel + ((lane8 % PIX) // P_SIZE).astype(F32) + 0.5
    weights = jnp.cos((90.0 - 0.25 * pixel) * (math.pi / 180.0))
    root = jnp.sqrt(weights)
    for r in range(BANDS):
        wq[pl.ds(r * COLS, COLS), :] = jnp.broadcast_to(root[r : r + 1], (COLS, LANES))
    if RP > ROWS:
        wq[pl.ds(ROWS, RP - ROWS), :] = jnp.zeros((RP - ROWS, LANES), F32)
        yal[pl.ds(ROWS, RP - ROWS), :] = jnp.zeros((RP - ROWS, LANES), F32)
    weight_part = jnp.sum(jnp.where(row8 < BANDS, weights, 0.0), axis=0, keepdims=True) * (
        float(COLS) / float(G)
    )
    y_copy.wait()
    grid_rows = BANDS * P_SIZE
    KT = SEL * grid_rows
    values = tgt[...]
    high = values.astype(BF16)
    low = (values - high.astype(F32)).astype(BF16)
    k_id = iota((KT, LANES), 0)
    n_id = iota((KT, LANES), 1)
    for r in range(BANDS):
        place = (
            ((k_id // grid_rows) == (n_id // PIX))
            & ((k_id % grid_rows) == (r * P_SIZE + (n_id % PIX) // P_SIZE))
        ).astype(F32).astype(BF16)
        dims = (((0,), (0,)), ((), ()))
        wide[...] = lax.dot_general(high, place, dims, preferred_element_type=F32) + lax.dot_general(
            low, place, dims, preferred_element_type=F32
        )
        aligned = jnp.zeros((COLS, LANES), F32)
        phase = iota((COLS, LANES), 1) % P_SIZE
        for j in range(P_SIZE):
            aligned = jnp.where(phase == j, wide[pl.ds(j, COLS, stride=P_SIZE), :], aligned)
        yal[pl.ds(r * COLS, COLS), :] = aligned
    rsum[...] = jnp.zeros(rsum.shape, F32)
    rsum[pl.ds(NBP - 1 if NBP > M + 1 else 0, 1), :] = weight_part
    wslot = NBP - 1 if NBP > M + 1 else 0

    for c in p1[:-1]:
        c.wait_send()

    x_c = []
    for o in range(1, X):
        for o2 in range(X):
            if o2 != o:
                part = fields.at[mem(me), chip_rows((xc + o2) % X)]
                c = remote(part, part, x_s.at[o, o2], x_r.at[o, o2], "member", ((xc + o) % X) * 2 + core)
                c.start()
                x_c.append((o, o2, c))
    for c in p1:
        c.wait_recv()
    pairs = [(a, b) for a in range(M) for b in range(a + 1, M + 1)]
    for first in range(0, len(pairs), 36):
        group = pairs[first : first + 36]
        used = sorted({a for pair in group for a in pair})

        def gap_step(k, sums, group=group, used=used):
            start = pl.multiple_of(me * CH + k * 16, 16)
            root_rows = wq[pl.ds(start, 16), :]
            loaded = {}
            for b in used:
                if b < M:
                    loaded[b] = fields[b, pl.ds(start, 16), :].astype(F32) * root_rows
                else:
                    loaded[b] = yal[pl.ds(start, 16), :] * root_rows
            sums = list(sums)
            for half in range(2):
                part = {b: loaded[b][half * 8 : half * 8 + 8] for b in used}
                for n, (a, b) in enumerate(group):
                    delta = part[a] - part[b]
                    sums[n] = sums[n] + delta * delta
            return tuple(sums)

        zero = jnp.zeros((8, LANES), F32)
        sums = lax.fori_loop(0, CH // 16, gap_step, tuple(zero for _ in group))
        for n, (a, b) in enumerate(group):
            line = jnp.sum(sums[n], axis=0, keepdims=True)
            rsum[pl.ds(a * NBP + b, 1), :] = line
            if b < M:
                rsum[pl.ds(b * NBP + a, 1), :] = line

    channel = (iota((SEL, LANES), 0) == iota((SEL, LANES), 1) // PIX).astype(F32)
    abuf[lat] = lax.dot_general(
        channel, rsum[...], (((1,), (1,)), ((), ())), precision=HIGH, preferred_element_type=F32
    )
    a_c = []
    for o in range(1, L):
        c = remote(abuf.at[lat], abuf.at[lat], a_s.at[o], a_r.at[o], "lat", (lat + o) % L)
        c.start()
        a_c.append(c)

    for c in i_c:
        c.start()
    ii_c = []
    for o in range(1, X):
        chip = (xc + o) % X
        part = fields.at[pl.ds(chip * (2 * LM), 2 * LM), chunk(me)]
        c = remote(part, part, ii_s.at[o], ii_r.at[o], "member", mate)
        c.start()
        ii_c.append(c)

    for c in a_c:
        c.wait_recv()
    total = abuf[0]
    for l in range(1, L):
        total = total + abuf[l]
    bbuf[me] = total
    b_c = []
    for o in range(1, G):
        c = remote(bbuf.at[me], bbuf.at[me], b_s.at[o], b_r.at[o], "member", (me + o) % G)
        c.start()
        b_c.append(c)
    iii_c = []
    for o, o2, c in x_c:
        c.wait_recv()
        chip = (xc + X - o) % X
        part = fields.at[mem(chip * 2 + core), chip_rows((chip + o2) % X)]
        q = remote(part, part, iii_s.at[o, o2], iii_r.at[o, o2], "member", mate)
        q.start()
        iii_c.append(q)

    for c in b_c:
        c.wait_recv()
    total = bbuf[0]
    for g in range(1, G):
        total = total + bbuf[g]

    pair_lane = iota((SEL, NL), 1)
    a_id = pair_lane // NBP
    b_id = pair_lane % NBP
    weight_sum = jnp.sum(jnp.where(pair_lane == wslot, total, 0.0), axis=1, keepdims=True)
    gap = jnp.where((b_id <= M) & (a_id != b_id), total / weight_sum, 0.0)
    distance = jnp.sqrt(jnp.abs(gap) + EPSILON)
    sign = jnp.where(gap > 0.0, 1.0, jnp.where(gap < 0.0, -1.0, 0.0))
    inverse = sign / distance
    share = jnp.where(b_id < M, -1.0 / (2.0 * M * M), jnp.where(b_id == M, 1.0 / M, 0.0))
    energy_ref[...] = jnp.sum(
        jnp.sum(distance * share, axis=1, keepdims=True), axis=0, keepdims=True
    )
    crow[...] = lax.dot_general(
        inverse, channel, (((0,), (0,)), ((), ())), precision=HIGH, preferred_element_type=F32
    )
    scale = float(M * BANDS * L * P_SIZE * COLS * P_SIZE)
    one_weight = weight_sum[0:1, :]
    b_row = iota((NBP, LANES), 0)
    coefs = []
    for lm in range(LM):
        m = me * LM + lm
        inv = crow[pl.ds(pl.multiple_of(m * NBP, 8), NBP), :]
        pair_terms = jnp.where(b_row < M, inv, 0.0) * (1.0 / (M * M))
        own_terms = inv[M : M + 1] * (1.0 / M)
        add = own_terms - jnp.sum(pair_terms, axis=0, keepdims=True)
        coef = pair_terms + jnp.where(b_row == m, add, 0.0) - jnp.where(b_row == M, own_terms, 0.0)
        coefs.append(coef * (scale / one_weight))

    for o in range(X):
        mate_own(o, mate).wait_recv()
    for c in ii_c:
        c.wait_recv()
    for c in iii_c:
        c.wait_recv()

    lines = [[coefs[lm][b : b + 1] for b in range(M + 1)] for lm in range(LM)]

    def combine(k, carry):
        start = pl.multiple_of(k * 16, 16)
        root_rows = wq[pl.ds(start, 16), :]
        row_weight = root_rows * root_rows
        stacked = [fields[b, pl.ds(start, 16), :].astype(F32) for b in range(M)]
        stacked.append(yal[pl.ds(start, 16), :])
        for lm in range(LM):
            acc = stacked[0] * lines[lm][0]
            for b in range(1, M + 1):
                acc = acc + stacked[b] * lines[lm][b]
            up[lm, pl.ds(start, 16), :] = (acc * row_weight).astype(BF16)
        return carry

    lax.fori_loop(0, RP // 16, combine, 0)
    for lm in range(LM):
        up_t[lm] = up[lm].T

    def head_block(d):
        cols = pl.ds(pl.multiple_of(d * DB, 128), DB)
        acc = jnp.dot(up_t[0], tok[0, :, cols], preferred_element_type=F32)
        for lm in range(1, LM):
            acc = acc + jnp.dot(up_t[lm], tok[lm, :, cols], preferred_element_type=F32)
        return acc.T

    theirs = []
    for o in list(range(1, X)) + [0]:
        s1[o] = head_block(((xc + o) % X) * 2 + 1 - core).astype(BF16)
        c = remote(s1.at[o], r1.at[o], r1_s.at[o], r1_r.at[o], "member", mate)
        c.start()
        theirs.append(c)
    r2_c = []

    def pieces(value, n):
        for l in range(L):
            s2[n, l] = value[l * SB : (l + 1) * SB].astype(BF16)

    def deliver(ox):
        for o in FAR if ox else [o for o in FAR if o]:
            l = (lat + o) % L
            c = pltpu.make_async_remote_copy(
                src_ref=s2.at[ox, l],
                dst_ref=r2.at[ox, o],
                send_sem=r2_s.at[ox, o],
                recv_sem=r2_r.at[ox, o],
                device_id={"member": ((xc + ox) % X) * 2 + core, "lat": l},
                device_id_type=pl.DeviceIdType.MESH,
            )
            c.start()
            r2_c.append((ox, o, c))

    FAR = sorted(range(L), key=lambda o: -min(o, L - o))
    for ox in range(1, X):
        block = head_block(((xc + ox) % X) * 2 + core)
        theirs[ox - 1].wait_recv()
        pieces(block + r1[ox].astype(F32), ox)
        deliver(ox)
    total_block = head_block(me)
    theirs[X - 1].wait_recv()
    total_block = total_block + r1[0].astype(F32)
    pieces(total_block, 0)
    deliver(0)
    for l in range(L):
        own[l] = total_block[l * SB : (l + 1) * SB]

    parts = 6 if ROWS % 96 == 0 else (3 if ROWS % 48 == 0 else 1)
    step = ROWS // parts

    def back(lm, n):
        rows = pl.ds(n * step, step)
        gout[lm, rows, :] = jnp.dot(
            up[lm, rows, :], head_t[...], preferred_element_type=F32
        ).astype(BF16)

    jobs = [(lm, n) for lm in range(LM) for n in range(parts)]
    cut = len(jobs) // 2
    for job in jobs[:cut]:
        back(*job)
    for job in jobs[cut:]:
        back(*job)
    result = own[lat]
    for ox, o, c in r2_c:
        c.wait_recv()
        result = result + r2[ox, o].astype(F32)
    token_total = M * BANDS * L * COLS
    gw_ref[...] = result * (1.0 / math.sqrt(float(token_total)))

    p1[-1].wait_send()
    for c in i_c + ii_c + iii_c + a_c + b_c + theirs + [c for _, _, c in r2_c]:
        c.wait_send()
    for _, _, c in x_c:
        c.wait_send()


def finish(parts, energy_in, gout, gw_in, energy_hbm, gtok_hbm, gw_hbm, sems):
    LM, ROWS, _ = gout.shape
    step = ROWS // parts
    copies = []
    for lm in range(LM):
        for n in range(parts):
            rows = pl.ds(n * step, step)
            c = pltpu.make_async_copy(
                gout.at[lm, rows], gtok_hbm.at[lm, rows], sems.at[lm * parts + n]
            )
            c.start()
            copies.append(c)
    for n, (src, dst) in enumerate([(energy_in, energy_hbm), (gw_in, gw_hbm)]):
        c = pltpu.make_async_copy(src, dst, sems.at[LM * parts + n])
        c.start()
        copies.append(c)
    for c in copies:
        c.wait()


def shards(tokens, weight, channels, band_rows, target):
    LM, BANDS, COLS, D = tokens.shape
    G = lax.axis_size("member")
    L = lax.axis_size("lat")
    X = G // 2
    M = G * LM
    ROWS = BANDS * COLS
    RP = round_up(ROWS, 16 * G)
    NBP = round_up(M + 1, 8)
    NL = M * NBP
    DB = D // G
    SB = DB // L
    KT = SEL * BANDS * P_SIZE
    dma = pltpu.SemaphoreType.DMA
    parts = 3 if ROWS % 48 == 0 else 1
    hbm = pl.BlockSpec(memory_space=pltpu.HBM)
    vmem = pl.BlockSpec(memory_space=pltpu.VMEM)
    energy, gout, grad_weight = pl.pallas_call(
        functools.partial(body, G, L, LM, BANDS, COLS),
        out_shape=(
            pltpu.VMEM((1, 1), F32),
            pltpu.VMEM((LM, ROWS, D), BF16),
            pltpu.VMEM((SB, LANES), F32),
        ),
        in_specs=[hbm, hbm, hbm, hbm, hbm],
        out_specs=(vmem, vmem, vmem),
        scratch_shapes=[
            pltpu.SMEM(channels.shape, jnp.int32),
            pltpu.SMEM(band_rows.shape, jnp.int32),
            pltpu.VMEM((LM, RP, D), BF16),
            pltpu.VMEM((weight.shape[1] // PIX, PIX, D), BF16),
            pltpu.VMEM((KT, COLS * P_SIZE), F32),
            pltpu.VMEM((COLS * P_SIZE, LANES), F32),
            pltpu.VMEM((RP, LANES), F32),
            pltpu.VMEM((RP, LANES), F32),
            pltpu.VMEM((M, RP, LANES), BF16),
            pltpu.VMEM((NL, LANES), F32),
            pltpu.VMEM((L, SEL, NL), F32),
            pltpu.VMEM((G, SEL, NL), F32),
            pltpu.VMEM((NL, LANES), F32),
            pltpu.VMEM((LM, RP, LANES), BF16),
            pltpu.VMEM((LANES, D), BF16),
            pltpu.VMEM((LM, LANES, RP), BF16),
            pltpu.VMEM((X, DB, LANES), BF16),
            pltpu.VMEM((X, DB, LANES), BF16),
            pltpu.VMEM((L, SB, LANES), F32),
            pltpu.VMEM((X, L, SB, LANES), BF16),
            pltpu.VMEM((X, L, SB, LANES), BF16),
            dma((4 + LM * G,)),
            dma((G,)),
            dma((G,)),
            dma((X, X)),
            dma((X, X)),
            dma((X,)),
            dma((X,)),
            dma((X,)),
            dma((X,)),
            dma((X, X)),
            dma((X, X)),
            dma((L,)),
            dma((L,)),
            dma((G,)),
            dma((G,)),
            dma((X,)),
            dma((X,)),
            dma((X, L)),
            dma((X, L)),
        ],
        compiler_params=pltpu.CompilerParams(
            collective_id=0, has_side_effects=True, vmem_limit_bytes=VMEM_LIMIT
        ),
    )(
        channels,
        band_rows,
        tokens.reshape(LM, ROWS, D),
        weight.T.reshape(weight.shape[1] // PIX, PIX, D),
        target.reshape(KT, COLS * P_SIZE),
    )
    energy, grad_tokens, grad_weight = pl.pallas_call(
        functools.partial(finish, parts),
        out_shape=(
            jax.ShapeDtypeStruct((1, 1), F32),
            jax.ShapeDtypeStruct((LM, ROWS, D), BF16),
            jax.ShapeDtypeStruct((SB, LANES), F32),
        ),
        in_specs=[vmem] * 3,
        out_specs=(hbm, hbm, hbm),
        scratch_shapes=[dma((LM * parts + 2,))],
        compiler_params=pltpu.CompilerParams(vmem_limit_bytes=4 * 1024 * 1024),
    )(energy, gout, grad_weight)
    return (energy.reshape(()), grad_tokens.reshape(tokens.shape), grad_weight)


def solution(mesh):
    placed = (P("member", "lat", None, None), P(), P(), P("lat"), P(None, "lat", None))
    return jax.shard_map(
        shards,
        mesh=mesh,
        in_specs=placed,
        out_specs=(P(), P("member", "lat", None, None), P(("member", "lat"), None)),
        check_vma=False,
    )
```

```python
import functools
import math

import jax
import jax.numpy as jnp
from jax import lax
from jax.experimental import pallas as pl
from jax.experimental.pallas import tpu as pltpu
from jax.sharding import PartitionSpec as P

SEL = 8
P_SIZE = 4
PIX = P_SIZE * P_SIZE
LANES = SEL * PIX
EPSILON = 0.0001
F32 = jnp.float32
BF16 = jnp.bfloat16
HIGH = lax.Precision.HIGHEST
VMEM_LIMIT = 121 * 512 * 1024


def round_up(value, step):
    return -(-value // step) * step


def iota(shape, axis):
    return lax.broadcasted_iota(jnp.int32, shape, axis)


def body(
    G,
    L,
    LM,
    BANDS,
    COLS,
    chan_hbm,
    band_hbm,
    tok_hbm,
    w_hbm,
    tgt_hbm,
    energy_ref,
    gout,
    gw_ref,
    chan_ref,
    band_ref,
    tok,
    wfull,
    tgt,
    wide,
    yal,
    wq,
    fields,
    rsum,
    abuf,
    bbuf,
    crow,
    up,
    head_t,
    up_t,
    s1,
    r1,
    own,
    s2,
    r2,
    ld_sem,
    p1_s,
    p1_r,
    x_s,
    x_r,
    i_s,
    i_r,
    ii_s,
    ii_r,
    iii_s,
    iii_r,
    a_s,
    a_r,
    b_s,
    b_r,
    r1_s,
    r1_r,
    r2_s,
    r2_r,
):
    X = G // 2
    M = G * LM
    ROWS = BANDS * COLS
    RP = fields.shape[1]
    CH = RP // G
    D = tok.shape[2]
    NBP = round_up(M + 1, 8)
    NL = M * NBP
    DB = D // G
    SB = DB // L
    me = lax.axis_index("member")
    lat = lax.axis_index("lat")
    xc = me // 2
    core = me % 2
    mate = me + 1 - 2 * core

    def dev(kind, index):
        return {kind: index}

    def remote(src, dst, ssem, rsem, kind, index):
        return pltpu.make_async_remote_copy(
            src_ref=src,
            dst_ref=dst,
            send_sem=ssem,
            recv_sem=rsem,
            device_id=dev(kind, index),
            device_id_type=pl.DeviceIdType.MESH,
        )

    barrier = pltpu.get_barrier_semaphore()
    for o in range(1, G):
        pl.semaphore_signal(
            barrier, inc=1, device_id=dev("member", (me + o) % G), device_id_type=pl.DeviceIdType.MESH
        )
    for o in range(1, L):
        for ox in range(X):
            pl.semaphore_signal(
                barrier,
                inc=1,
                device_id={"member": ((xc + ox) % X) * 2 + core, "lat": (lat + o) % L},
                device_id_type=pl.DeviceIdType.MESH,
            )

    w_copy = pltpu.make_async_copy(w_hbm, wfull, ld_sem.at[0])
    w_copy.start()
    c_copy = pltpu.make_async_copy(chan_hbm, chan_ref, ld_sem.at[2 + LM * G])
    c_copy.start()
    r_copy = pltpu.make_async_copy(band_hbm, band_ref, ld_sem.at[3 + LM * G])
    r_copy.start()
    t_copies = []
    for g in range(G):
        for lm in range(LM):
            rows = pl.ds(g * CH, min(CH, ROWS - g * CH))
            c = pltpu.make_async_copy(
                tok_hbm.at[lm, rows], tok.at[lm, rows], ld_sem.at[2 + g * LM + lm]
            )
            c.start()
            t_copies.append(c)
    y_copy = pltpu.make_async_copy(tgt_hbm, tgt, ld_sem.at[1])
    y_copy.start()

    if RP > ROWS:
        for lm in range(LM):
            tok[lm, pl.ds(ROWS, RP - ROWS), :] = jnp.zeros((RP - ROWS, D), BF16)
    c_copy.wait()
    r_copy.wait()
    w_copy.wait()
    for s in range(SEL):
        head_t[pl.ds(s * PIX, PIX), :] = wfull[chan_ref[s]]
    for c in t_copies:
        c.wait()
    pl.semaphore_wait(barrier, G - 1 + (L - 1) * X)

    def chunk(index):
        return pl.ds(pl.multiple_of(index * CH, 16), CH)

    def chip_rows(index):
        return pl.ds(pl.multiple_of(index * (2 * CH), 16), 2 * CH)

    def mem(device):
        return pl.ds(device * LM, LM)

    def predict(d):
        for lm in range(LM):
            fields[me * LM + lm, chunk(d), :] = lax.dot_general(
                tok[lm, chunk(d), :],
                head_t[...],
                (((1,), (1,)), ((), ())),
                preferred_element_type=F32,
            ).astype(BF16)

    p1 = []
    for o in [o for o in range(2, G)] + [1]:
        if o == 1:
            d = mate
        else:
            d = ((xc + o // 2) % X) * 2 + (core + o % 2) % 2
        predict(d)
        part = fields.at[mem(me), chunk(d)]
        c = remote(part, part, p1_s.at[o], p1_r.at[o], "member", d)
        c.start()
        p1.append(c)
    predict(me)

    def mate_own(o, owner):
        rows = chunk(owner) if o == 0 else chip_rows((xc + o) % X)
        part = fields.at[mem(owner), rows]
        return remote(part, part, i_s.at[o], i_r.at[o], "member", mate)

    i_c = [mate_own(o, me) for o in range(X)]

    lane8 = iota((8, LANES), 1)
    row8 = iota((8, LANES), 0)
    pixel = jnp.zeros((8, LANES), F32)
    for r in range(BANDS):
        pixel = jnp.where(row8 == r, band_ref[r].astype(F32) * P_SIZE, pixel)
    pixel = pixel + ((lane8 % PIX) // P_SIZE).astype(F32) + 0.5
    weights = jnp.cos((90.0 - 0.25 * pixel) * (math.pi / 180.0))
    root = jnp.sqrt(weights)
    for r in range(BANDS):
        wq[pl.ds(r * COLS, COLS), :] = jnp.broadcast_to(root[r : r + 1], (COLS, LANES))
    if RP > ROWS:
        wq[pl.ds(ROWS, RP - ROWS), :] = jnp.zeros((RP - ROWS, LANES), F32)
        yal[pl.ds(ROWS, RP - ROWS), :] = jnp.zeros((RP - ROWS, LANES), F32)
    weight_part = jnp.sum(jnp.where(row8 < BANDS, weights, 0.0), axis=0, keepdims=True) * (
        float(COLS) / float(G)
    )
    y_copy.wait()
    grid_rows = BANDS * P_SIZE
    KT = SEL * grid_rows
    values = tgt[...]
    high = values.astype(BF16)
    low = (values - high.astype(F32)).astype(BF16)
    k_id = iota((KT, LANES), 0)
    n_id = iota((KT, LANES), 1)
    for r in range(BANDS):
        place = (
            ((k_id // grid_rows) == (n_id // PIX))
            & ((k_id % grid_rows) == (r * P_SIZE + (n_id % PIX) // P_SIZE))
        ).astype(F32).astype(BF16)
        dims = (((0,), (0,)), ((), ()))
        wide[...] = lax.dot_general(high, place, dims, preferred_element_type=F32) + lax.dot_general(
            low, place, dims, preferred_element_type=F32
        )
        aligned = jnp.zeros((COLS, LANES), F32)
        phase = iota((COLS, LANES), 1) % P_SIZE
        for j in range(P_SIZE):
            aligned = jnp.where(phase == j, wide[pl.ds(j, COLS, stride=P_SIZE), :], aligned)
        yal[pl.ds(r * COLS, COLS), :] = aligned
    rsum[...] = jnp.zeros(rsum.shape, F32)
    rsum[pl.ds(NBP - 1 if NBP > M + 1 else 0, 1), :] = weight_part
    wslot = NBP - 1 if NBP > M + 1 else 0

    for c in p1[:-1]:
        c.wait_send()
    for c in p1:
        c.wait_recv()

    x_c = []
    for o in range(1, X):
        for o2 in range(X):
            if o2 != o:
                part = fields.at[mem(me), chip_rows((xc + o2) % X)]
                c = remote(part, part, x_s.at[o, o2], x_r.at[o, o2], "member", ((xc + o) % X) * 2 + core)
                c.start()
                x_c.append((o, o2, c))
    pairs = [(a, b) for a in range(M) for b in range(a + 1, M + 1)]
    for first in range(0, len(pairs), 36):
        group = pairs[first : first + 36]
        used = sorted({a for pair in group for a in pair})

        def gap_step(k, sums, group=group, used=used):
            start = pl.multiple_of(me * CH + k * 16, 16)
            root_rows = wq[pl.ds(start, 16), :]
            loaded = {}
            for b in used:
                if b < M:
                    loaded[b] = fields[b, pl.ds(start, 16), :].astype(F32) * root_rows
                else:
                    loaded[b] = yal[pl.ds(start, 16), :] * root_rows
            sums = list(sums)
            for half in range(2):
                part = {b: loaded[b][half * 8 : half * 8 + 8] for b in used}
                for n, (a, b) in enumerate(group):
                    delta = part[a] - part[b]
                    sums[n] = sums[n] + delta * delta
            return tuple(sums)

        zero = jnp.zeros((8, LANES), F32)
        sums = lax.fori_loop(0, CH // 16, gap_step, tuple(zero for _ in group))
        for n, (a, b) in enumerate(group):
            line = jnp.sum(sums[n], axis=0, keepdims=True)
            rsum[pl.ds(a * NBP + b, 1), :] = line
            if b < M:
                rsum[pl.ds(b * NBP + a, 1), :] = line

    channel = (iota((SEL, LANES), 0) == iota((SEL, LANES), 1) // PIX).astype(F32)
    abuf[lat] = lax.dot_general(
        channel, rsum[...], (((1,), (1,)), ((), ())), precision=HIGH, preferred_element_type=F32
    )
    a_c = []
    for o in sorted(range(1, L), key=lambda o: -min(o, L - o)):
        c = remote(abuf.at[lat], abuf.at[lat], a_s.at[o], a_r.at[o], "lat", (lat + o) % L)
        c.start()
        a_c.append(c)

    for c in i_c:
        c.start()
    ii_c = []
    for o in range(1, X):
        chip = (xc + o) % X
        part = fields.at[pl.ds(chip * (2 * LM), 2 * LM), chunk(me)]
        c = remote(part, part, ii_s.at[o], ii_r.at[o], "member", mate)
        c.start()
        ii_c.append(c)

    for c in a_c:
        c.wait_recv()
    total = abuf[0]
    for l in range(1, L):
        total = total + abuf[l]
    bbuf[me] = total
    b_c = []
    for o in range(1, G):
        c = remote(bbuf.at[me], bbuf.at[me], b_s.at[o], b_r.at[o], "member", (me + o) % G)
        c.start()
        b_c.append(c)
    iii_c = []
    for o, o2, c in x_c:
        c.wait_recv()
        chip = (xc + X - o) % X
        part = fields.at[mem(chip * 2 + core), chip_rows((chip + o2) % X)]
        q = remote(part, part, iii_s.at[o, o2], iii_r.at[o, o2], "member", mate)
        q.start()
        iii_c.append(q)

    for c in b_c:
        c.wait_recv()
    total = bbuf[0]
    for g in range(1, G):
        total = total + bbuf[g]

    pair_lane = iota((SEL, NL), 1)
    a_id = pair_lane // NBP
    b_id = pair_lane % NBP
    weight_sum = jnp.sum(jnp.where(pair_lane == wslot, total, 0.0), axis=1, keepdims=True)
    gap = jnp.where((b_id <= M) & (a_id != b_id), total / weight_sum, 0.0)
    distance = jnp.sqrt(jnp.abs(gap) + EPSILON)
    sign = jnp.where(gap > 0.0, 1.0, jnp.where(gap < 0.0, -1.0, 0.0))
    inverse = sign / distance
    share = jnp.where(b_id < M, -1.0 / (2.0 * M * M), jnp.where(b_id == M, 1.0 / M, 0.0))
    energy_ref[...] = jnp.sum(
        jnp.sum(distance * share, axis=1, keepdims=True), axis=0, keepdims=True
    )
    crow[...] = lax.dot_general(
        inverse, channel, (((0,), (0,)), ((), ())), precision=HIGH, preferred_element_type=F32
    )
    scale = float(M * BANDS * L * P_SIZE * COLS * P_SIZE)
    one_weight = weight_sum[0:1, :]
    b_row = iota((NBP, LANES), 0)
    coefs = []
    for lm in range(LM):
        m = me * LM + lm
        inv = crow[pl.ds(pl.multiple_of(m * NBP, 8), NBP), :]
        pair_terms = jnp.where(b_row < M, inv, 0.0) * (1.0 / (M * M))
        own_terms = inv[M : M + 1] * (1.0 / M)
        add = own_terms - jnp.sum(pair_terms, axis=0, keepdims=True)
        coef = pair_terms + jnp.where(b_row == m, add, 0.0) - jnp.where(b_row == M, own_terms, 0.0)
        coefs.append(coef * (scale / one_weight))

    for o in range(X):
        mate_own(o, mate).wait_recv()
    for c in ii_c:
        c.wait_recv()
    for c in iii_c:
        c.wait_recv()

    lines = [[coefs[lm][b : b + 1] for b in range(M + 1)] for lm in range(LM)]

    def combine(k, carry):
        start = pl.multiple_of(k * 16, 16)
        root_rows = wq[pl.ds(start, 16), :]
        row_weight = root_rows * root_rows
        stacked = [fields[b, pl.ds(start, 16), :].astype(F32) for b in range(M)]
        stacked.append(yal[pl.ds(start, 16), :])
        for lm in range(LM):
            acc = stacked[0] * lines[lm][0]
            for b in range(1, M + 1):
                acc = acc + stacked[b] * lines[lm][b]
            up[lm, pl.ds(start, 16), :] = (acc * row_weight).astype(BF16)
        return carry

    lax.fori_loop(0, RP // 16, combine, 0)
    for lm in range(LM):
        up_t[lm] = up[lm].T

    def head_block(d):
        cols = pl.ds(pl.multiple_of(d * DB, 128), DB)
        acc = jnp.dot(up_t[0], tok[0, :, cols], preferred_element_type=F32)
        for lm in range(1, LM):
            acc = acc + jnp.dot(up_t[lm], tok[lm, :, cols], preferred_element_type=F32)
        return acc.T

    theirs = []
    for o in list(range(1, X)) + [0]:
        s1[o] = head_block(((xc + o) % X) * 2 + 1 - core).astype(BF16)
        c = remote(s1.at[o], r1.at[o], r1_s.at[o], r1_r.at[o], "member", mate)
        c.start()
        theirs.append(c)
    r2_c = []

    def pieces(value, n):
        for l in range(L):
            s2[n, l] = value[l * SB : (l + 1) * SB].astype(BF16)

    def deliver(ox):
        for o in FAR if ox else [o for o in FAR if o]:
            l = (lat + o) % L
            c = pltpu.make_async_remote_copy(
                src_ref=s2.at[ox, l],
                dst_ref=r2.at[ox, o],
                send_sem=r2_s.at[ox, o],
                recv_sem=r2_r.at[ox, o],
                device_id={"member": ((xc + ox) % X) * 2 + core, "lat": l},
                device_id_type=pl.DeviceIdType.MESH,
            )
            c.start()
            r2_c.append((ox, o, c))

    FAR = sorted(range(L), key=lambda o: -min(o, L - o))
    for ox in range(1, X):
        block = head_block(((xc + ox) % X) * 2 + core)
        theirs[ox - 1].wait_recv()
        pieces(block + r1[ox].astype(F32), ox)
        deliver(ox)
    total_block = head_block(me)
    theirs[X - 1].wait_recv()
    total_block = total_block + r1[0].astype(F32)
    pieces(total_block, 0)
    deliver(0)
    for l in range(L):
        own[l] = total_block[l * SB : (l + 1) * SB]

    parts = 6 if ROWS % 96 == 0 else (3 if ROWS % 48 == 0 else 1)
    step = ROWS // parts

    def back(lm, n):
        rows = pl.ds(n * step, step)
        gout[lm, rows, :] = jnp.dot(
            up[lm, rows, :], head_t[...], preferred_element_type=F32
        ).astype(BF16)

    jobs = [(lm, n) for lm in range(LM) for n in range(parts)]
    cut = len(jobs) // 2
    for job in jobs[:cut]:
        back(*job)
    for job in jobs[cut:]:
        back(*job)
    result = own[lat]
    for ox, o, c in r2_c:
        c.wait_recv()
        result = result + r2[ox, o].astype(F32)
    token_total = M * BANDS * L * COLS
    gw_ref[...] = result * (1.0 / math.sqrt(float(token_total)))

    p1[-1].wait_send()
    for c in i_c + ii_c + iii_c + a_c + b_c + theirs + [c for _, _, c in r2_c]:
        c.wait_send()
    for _, _, c in x_c:
        c.wait_send()


def finish(parts, energy_in, gout, gw_in, energy_hbm, gtok_hbm, gw_hbm, sems):
    LM, ROWS, _ = gout.shape
    step = ROWS // parts
    copies = []
    for lm in range(LM):
        for n in range(parts):
            rows = pl.ds(n * step, step)
            c = pltpu.make_async_copy(
                gout.at[lm, rows], gtok_hbm.at[lm, rows], sems.at[lm * parts + n]
            )
            c.start()
            copies.append(c)
    for n, (src, dst) in enumerate([(energy_in, energy_hbm), (gw_in, gw_hbm)]):
        c = pltpu.make_async_copy(src, dst, sems.at[LM * parts + n])
        c.start()
        copies.append(c)
    for c in copies:
        c.wait()


def shards(tokens, weight, channels, band_rows, target):
    LM, BANDS, COLS, D = tokens.shape
    G = lax.axis_size("member")
    L = lax.axis_size("lat")
    X = G // 2
    M = G * LM
    ROWS = BANDS * COLS
    RP = round_up(ROWS, 16 * G)
    NBP = round_up(M + 1, 8)
    NL = M * NBP
    DB = D // G
    SB = DB // L
    KT = SEL * BANDS * P_SIZE
    dma = pltpu.SemaphoreType.DMA
    parts = 1
    hbm = pl.BlockSpec(memory_space=pltpu.HBM)
    vmem = pl.BlockSpec(memory_space=pltpu.VMEM)
    energy, gout, grad_weight = pl.pallas_call(
        functools.partial(body, G, L, LM, BANDS, COLS),
        out_shape=(
            pltpu.VMEM((1, 1), F32),
            pltpu.VMEM((LM, ROWS, D), BF16),
            pltpu.VMEM((SB, LANES), F32),
        ),
        in_specs=[hbm, hbm, hbm, hbm, hbm],
        out_specs=(vmem, vmem, vmem),
        scratch_shapes=[
            pltpu.SMEM(channels.shape, jnp.int32),
            pltpu.SMEM(band_rows.shape, jnp.int32),
            pltpu.VMEM((LM, RP, D), BF16),
            pltpu.VMEM((weight.shape[1] // PIX, PIX, D), BF16),
            pltpu.VMEM((KT, COLS * P_SIZE), F32),
            pltpu.VMEM((COLS * P_SIZE, LANES), F32),
            pltpu.VMEM((RP, LANES), F32),
            pltpu.VMEM((RP, LANES), F32),
            pltpu.VMEM((M, RP, LANES), BF16),
            pltpu.VMEM((NL, LANES), F32),
            pltpu.VMEM((L, SEL, NL), F32),
            pltpu.VMEM((G, SEL, NL), F32),
            pltpu.VMEM((NL, LANES), F32),
            pltpu.VMEM((LM, RP, LANES), BF16),
            pltpu.VMEM((LANES, D), BF16),
            pltpu.VMEM((LM, LANES, RP), BF16),
            pltpu.VMEM((X, DB, LANES), BF16),
            pltpu.VMEM((X, DB, LANES), BF16),
            pltpu.VMEM((L, SB, LANES), F32),
            pltpu.VMEM((X, L, SB, LANES), BF16),
            pltpu.VMEM((X, L, SB, LANES), BF16),
            dma((4 + LM * G,)),
            dma((G,)),
            dma((G,)),
            dma((X, X)),
            dma((X, X)),
            dma((X,)),
            dma((X,)),
            dma((X,)),
            dma((X,)),
            dma((X, X)),
            dma((X, X)),
            dma((L,)),
            dma((L,)),
            dma((G,)),
            dma((G,)),
            dma((X,)),
            dma((X,)),
            dma((X, L)),
            dma((X, L)),
        ],
        compiler_params=pltpu.CompilerParams(
            collective_id=0, has_side_effects=True, vmem_limit_bytes=VMEM_LIMIT
        ),
    )(
        channels,
        band_rows,
        tokens.reshape(LM, ROWS, D),
        weight.T.reshape(weight.shape[1] // PIX, PIX, D),
        target.reshape(KT, COLS * P_SIZE),
    )
    energy, grad_tokens, grad_weight = pl.pallas_call(
        functools.partial(finish, parts),
        out_shape=(
            jax.ShapeDtypeStruct((1, 1), F32),
            jax.ShapeDtypeStruct((LM, ROWS, D), BF16),
            jax.ShapeDtypeStruct((SB, LANES), F32),
        ),
        in_specs=[vmem] * 3,
        out_specs=(hbm, hbm, hbm),
        scratch_shapes=[dma((LM * parts + 2,))],
        compiler_params=pltpu.CompilerParams(vmem_limit_bytes=4 * 1024 * 1024),
    )(energy, gout, grad_weight)
    return (energy.reshape(()), grad_tokens.reshape(tokens.shape), grad_weight)


def solution(mesh):
    placed = (P("member", "lat", None, None), P(), P(), P("lat"), P(None, "lat", None))
    return jax.shard_map(
        shards,
        mesh=mesh,
        in_specs=placed,
        out_specs=(P(), P("member", "lat", None, None), P(("member", "lat"), None)),
        check_vma=False,
    )
```
